256 devices in a mesh: dp: 32 (over z, x), vocab: 8 (over y, core).
Axes of the slice: x: 4, y: 4, z: 8, core: 2. Of those that a mesh axis runs over, the one named last changes fastest.
Arguments:
- slot_word: int32 [1024, 128], P('dp', 'vocab'), may hold values from 0 to 2047
- slot_doc: int32 [1024, 128], P('dp', 'vocab'), may hold values from 0 to 63
- slot_count: int32 [1024, 128], P('dp', 'vocab'), may hold values from 0 to 4
- resp_weight: bfloat16 [1024, 128, 1024], P('dp', 'vocab'), may hold values from 0.099 to 10
Outputs:
- resp_new: bfloat16 [1024, 128, 1024], P('dp', 'vocab')
- word_topic: float32 [524288, 1024], P(('dp', 'vocab'))
- doc_topic: float32 [2048, 1024], P('dp')
The draws below stay inside these ranges and needn't reach their ends.
All inputs are finite; a program needn't handle non-finite values.
Results may differ from the reference program's by a relative error of at most 0.0012.
Values may be sent and summed in bfloat16 or wider, within the bound.
No kernel may reach another device: no remote copies, remote signals or barrier semaphores. Data moves between devices by JAX's collectives and lax.ppermute only.
A program may use at most 64 MiB of HBM per device.

```python
import math
import jax
import jax.numpy as jnp
import numpy as np
from jax import lax

K = 1024
VOC_DEV = 2048
SLOTS = 16
DOCS = 64
ROWS = 1024
COLS = 128
WORDS = 524288
DOCS_ALL = 2048
N_DP = 32
N_VOCAB = 8


def draw_resp_weight(key, part):
    key = jax.random.fold_in(key, 7)
    keys = jax.random.split(key, 5)
    blocks = 8
    width = K // blocks
    topic_level = jax.random.uniform(keys[0], (blocks,), jnp.float32, -0.6, 0.6)
    shard_level = jax.random.uniform(keys[1], (N_DP, blocks), jnp.float32, -0.4, 0.4)
    column_level = jax.random.uniform(keys[2], (N_VOCAB, blocks), jnp.float32, -0.4, 0.4)
    fine_level = jax.random.uniform(keys[3], (K,), jnp.float32, -0.3, 0.3)
    level = topic_level[None, None, :] + shard_level[:, None, :] + column_level[None, :, :]
    level = jnp.repeat(level, width, axis=2) + fine_level[None, None, :]
    full_shape = (N_DP, N_DP, N_VOCAB, SLOTS, K)
    element = jax.random.uniform(keys[4], full_shape, jnp.float32, -0.6, 0.6)
    exponent = jnp.clip(element + level[:, None, :, None, :], -1.0, 1.0)
    return jnp.power(10.0, exponent).reshape(ROWS, COLS, K).astype(jnp.bfloat16)


def with_ends(entries, stream_key, smallest, largest):
    place = [jax.random.randint(jax.random.fold_in(stream_key, axis), (), 0, length) for axis, length in enumerate(entries.shape)]
    longest = entries.shape.index(max(entries.shape))
    neighbour = place[:longest] + [(place[longest] + 1) % entries.shape[longest]] + place[longest + 1:]
    return entries.at[tuple(place)].set(smallest).at[tuple(neighbour)].set(largest)


def rank_bounds(amount, slope):
    weights = [(1 << 20) // math.isqrt(grade ** slope) + 1 for grade in range(1, amount + 1)]
    deviation = 1 + sum(weights) // (1 << 30)
    return np.cumsum(np.array([max(1, weight // deviation) for weight in weights]))


def skewed_ids(own_key, shape, number_of, slope):
    table = rank_bounds(number_of, slope)
    ticket = jax.random.randint(jax.random.fold_in(own_key, 1), shape, 0, int(table[number_of - 1]))
    standing = jnp.searchsorted(jnp.asarray(table, jnp.int32), ticket, side="right")
    return jax.random.permutation(jax.random.fold_in(own_key, 2), number_of)[standing].astype(jnp.int32)


def setup_inputs(seed: int = 0) -> dict:
    splits = jax.random.split(jax.random.key(seed), 5)
    slot_word = with_ends(skewed_ids(splits[0], (ROWS, COLS), VOC_DEV, 2), jax.random.fold_in(splits[0], 3), 0, VOC_DEV - 1).astype(jnp.int32)
    slot_doc = with_ends(skewed_ids(splits[1], (ROWS, COLS), DOCS, 1), jax.random.fold_in(splits[1], 3), 0, DOCS - 1).astype(jnp.int32)
    slot_count = with_ends(jax.random.randint(splits[2], (ROWS, COLS), 0, 5), jax.random.fold_in(splits[2], 1), 0, 4).astype(jnp.int32)
    resp_weight = draw_resp_weight(jax.random.fold_in(splits[4], 71), 0)
    return {"slot_word": slot_word, "slot_doc": slot_doc, "slot_count": slot_count, "resp_weight": resp_weight}


def shares_of(weight, count):
    weight = weight.astype(jnp.float32)
    gamma = weight / jnp.sum(weight, axis=-1, keepdims=True)
    return count.astype(jnp.float32)[..., None] * gamma


def reference(slot_word, slot_doc, slot_count, resp_weight):
    weight_five = resp_weight.reshape(N_DP, N_DP, N_VOCAB, SLOTS, K)
    word_five = slot_word.reshape(N_DP, N_DP, N_VOCAB, SLOTS)
    count_five = slot_count.reshape(N_DP, N_DP, N_VOCAB, SLOTS)
    block_base = (jnp.arange(N_VOCAB, dtype=jnp.int32) * VOC_DEV)[None, :, None]

    def owner_block(owner):
        weight = lax.dynamic_index_in_dim(weight_five, owner, 1, keepdims=False)
        count = lax.dynamic_index_in_dim(count_five, owner, 1, keepdims=False)
        words = lax.dynamic_index_in_dim(word_five, owner, 1, keepdims=False)
        share = shares_of(weight, count)
        index = (block_base + words).astype(jnp.int32)
        return jax.ops.segment_sum(share.reshape(-1, K), index.reshape(-1), num_segments=N_VOCAB * VOC_DEV)

    word_topic = lax.map(owner_block, jnp.arange(N_DP, dtype=jnp.int32)).reshape(WORDS, K)

    weight_four = resp_weight.reshape(N_DP, N_DP, COLS, K)
    word_three = slot_word.reshape(N_DP, N_DP, COLS)
    doc_three = slot_doc.reshape(N_DP, N_DP, COLS)
    count_three = slot_count.reshape(N_DP, N_DP, COLS)

    def doc_block(index):
        share = shares_of(weight_four[index], count_three[index])
        return jax.ops.segment_sum(share.reshape(-1, K), doc_three[index].reshape(-1), num_segments=DOCS)

    doc_topic = lax.map(doc_block, jnp.arange(N_DP, dtype=jnp.int32)).reshape(DOCS_ALL, K)
    totals = jnp.sum(doc_topic, axis=0)
    owner_ids = jnp.arange(N_DP, dtype=jnp.int32)[:, None]
    column_block = (jnp.arange(COLS, dtype=jnp.int32) // SLOTS)[None, :]

    def new_block(index):
        share = shares_of(weight_four[index], count_three[index])
        global_word = ((owner_ids * N_VOCAB + column_block) * VOC_DEV + word_three[index]).astype(jnp.int32)
        word_rows = jnp.take(word_topic, global_word, axis=0)
        doc_rows = jnp.take(doc_topic, (index * DOCS + doc_three[index]).astype(jnp.int32), axis=0)
        raw = (word_rows - share + 0.01) * (doc_rows - share + 0.1) / (totals - share + 0.01 * WORDS)
        return (raw / jnp.sum(raw, axis=-1, keepdims=True)).astype(jnp.bfloat16)

    resp_new = lax.map(new_block, jnp.arange(N_DP, dtype=jnp.int32)).reshape(ROWS, COLS, K)
    return resp_new, word_topic, doc_topic
```

```python
import math

import jax
import jax.numpy as jnp
from jax import lax
from jax.experimental import pallas as pl
from jax.experimental.pallas import tpu as pltpu
from jax.sharding import PartitionSpec as P

VOC_DEV = 2048
DOCS = 64
BF = jnp.bfloat16
F32 = jnp.float32
ALPHA = 0.1
BETA = 0.01
CODES = 65535


def code_range(slots, topics):
    most = BETA + 4.0 * slots * (10.2 / (10.2 + (topics - 1) * 0.0985))
    low, high = math.log2(BETA) - 1e-3, math.log2(most) + 1e-3
    step = (high - low) / (CODES - 1)
    return step, low + (CODES // 2) * step


def dot(a, b):
    return jnp.dot(a, b, preferred_element_type=F32)


def split(x):
    high = x.astype(BF)
    return high, (x - high.astype(F32)).astype(BF)


def scale_row(weight_ref, count_row):
    ones = jnp.ones((8, weight_ref.shape[1]), BF)
    total = lax.dot_general(ones, weight_ref[...], (((1,), (1,)), ((), ())), preferred_element_type=F32)
    return count_row.astype(F32) / total


def doc_kernel(doc_ref, count_ref, weight_ref, out_ref, scale_ref):
    scale = scale_row(weight_ref, count_ref[...])
    scale_ref[...] = scale
    slots = scale.shape[1]
    ids = lax.broadcasted_iota(jnp.int32, (DOCS, slots), 0)
    picked = jnp.where(ids == doc_ref[...], scale[0:1], 0.0)
    high, low = split(picked)
    out_ref[...] = dot(high, weight_ref[...]) + dot(low, weight_ref[...])


def owner_kernel(step, middle, meta_ref, weight_ref, code_ref, scale_ref):
    meta = meta_ref[...]
    slots = meta.shape[1]
    scale = scale_row(weight_ref, meta & 7)
    scale_ref[...] = scale
    word = jnp.broadcast_to(meta >> 3, (8, slots))
    word_column = jnp.transpose(word)[:, 0:1]
    rows = lax.broadcasted_iota(jnp.int32, (slots, slots), 0)
    columns = lax.broadcasted_iota(jnp.int32, (slots, slots), 1)
    others = (word_column == word[0:1]) & (rows != columns)
    high, low = split(jnp.where(others, scale[0:1], 0.0))
    width = 256

    def part(i, _):
        at = pl.ds(pl.multiple_of(i * width, width), width)
        weight = weight_ref[:, at]
        value = dot(high, weight) + dot(low, weight) + BETA
        code = (jnp.log2(value) - middle) * (1.0 / step)
        code_ref[:, at] = jnp.round(code).astype(jnp.int32).astype(jnp.int16)
        return 0

    lax.fori_loop(0, weight_ref.shape[1] // width, part, 0)


def word_kernel(meta_ref, scale_ref, weight_ref, out_ref):
    rows, slots = out_ref.shape[0], meta_ref.shape[1]
    ids = lax.broadcasted_iota(jnp.int32, (rows, slots), 0) + pl.program_id(0) * rows
    high, low = split(jnp.where(ids == (meta_ref[...] >> 3), scale_ref[0:1], 0.0))
    out_ref[...] = dot(high, weight_ref[...]) + dot(low, weight_ref[...])


def new_kernel(step, middle, beta_all, doc_ref, scale_ref, code_ref, weight_ref, doc_topic_ref, totals_ref, out_ref):
    slots = doc_ref.shape[1]
    scale = jnp.transpose(scale_ref[...])[:, 0:1]
    ids = lax.broadcasted_iota(jnp.int32, (DOCS, slots), 0)
    picked = jnp.transpose((ids == doc_ref[...]).astype(F32)).astype(BF)
    doc_high, doc_low = split(doc_topic_ref[...])
    doc_rows = dot(picked, doc_high) + dot(picked, doc_low) + ALPHA
    share = scale * weight_ref[...].astype(F32)
    word_rows = jnp.exp2(code_ref[...].astype(jnp.int32).astype(F32) * step + middle)
    raw = word_rows * (doc_rows - share) / (totals_ref[...] + beta_all - share)
    norm = 1.0 / jnp.sum(raw, axis=-1, keepdims=True)
    out_ref[...] = (raw * norm).astype(BF)


def cost(flops, nbytes):
    return pl.CostEstimate(flops=flops, bytes_accessed=nbytes, transcendentals=0)


def on_device(slot_word, slot_doc, slot_count, resp_weight):
    owners, slots, topics = resp_weight.shape
    flat = owners * slots
    vocab_total = VOC_DEV * lax.axis_size("dp") * lax.axis_size("vocab")
    step, middle = code_range(flat, topics)
    params = pltpu.CompilerParams(vmem_limit_bytes=48 * 1024 * 1024)

    weight = resp_weight.reshape(flat, topics)
    doc_row = slot_doc.reshape(1, flat)
    count_row = slot_count.reshape(1, flat)
    arrived = lax.all_to_all(resp_weight, "dp", split_axis=0, concat_axis=0, tiled=True).reshape(flat, topics)
    meta = lax.all_to_all(slot_word * 8 + slot_count, "dp", split_axis=0, concat_axis=0, tiled=True).reshape(1, flat)

    doc_partial, scale = pl.pallas_call(
        doc_kernel,
        out_shape=(jax.ShapeDtypeStruct((DOCS, topics), F32), jax.ShapeDtypeStruct((8, flat), F32)),
        compiler_params=params,
        cost_estimate=cost(2 * 2 * DOCS * flat * topics, 2 * flat * topics),
        name="doc_counts",
    )(doc_row, count_row, weight)
    doc_topic = lax.psum(doc_partial, "vocab")
    totals = lax.psum(jnp.sum(doc_topic, axis=0, keepdims=True), "dp")

    code, owned_scale = pl.pallas_call(
        lambda *refs: owner_kernel(step, middle, *refs),
        out_shape=(jax.ShapeDtypeStruct((flat, topics), jnp.int16), jax.ShapeDtypeStruct((8, flat), F32)),
        compiler_params=params,
        cost_estimate=cost(2 * 2 * flat * flat * topics, 4 * flat * topics),
        name="word_rows",
    )(meta, arrived)
    returned = lax.all_to_all(
        code.reshape(owners, slots, topics), "dp", split_axis=0, concat_axis=0, tiled=True
    ).reshape(flat, topics)

    block = 256
    word_topic = pl.pallas_call(
        word_kernel,
        out_shape=jax.ShapeDtypeStruct((VOC_DEV, topics), F32),
        grid=(VOC_DEV // block,),
        in_specs=[
            pl.BlockSpec((1, flat), lambda i: (0, 0)),
            pl.BlockSpec((8, flat), lambda i: (0, 0)),
            pl.BlockSpec((flat, topics), lambda i: (0, 0)),
        ],
        out_specs=pl.BlockSpec((block, topics), lambda i: (i, 0)),
        compiler_params=params,
        cost_estimate=cost(2 * 2 * VOC_DEV * flat * topics, 4 * VOC_DEV * topics),
        name="word_counts",
    )(meta, owned_scale, arrived)

    rows = 128
    resp_new = pl.pallas_call(
        lambda *refs: new_kernel(step, middle, BETA * vocab_total, *refs),
        out_shape=jax.ShapeDtypeStruct((flat, topics), BF),
        grid=(flat // rows,),
        in_specs=[
            pl.BlockSpec((1, rows), lambda i: (0, i)),
            pl.BlockSpec((8, rows), lambda i: (0, i)),
            pl.BlockSpec((rows, topics), lambda i: (i, 0)),
            pl.BlockSpec((rows, topics), lambda i: (i, 0)),
            pl.BlockSpec((DOCS, topics), lambda i: (0, 0)),
            pl.BlockSpec((1, topics), lambda i: (0, 0)),
        ],
        out_specs=pl.BlockSpec((rows, topics), lambda i: (i, 0)),
        compiler_params=params,
        cost_estimate=cost(2 * 2 * DOCS * flat * topics, 6 * flat * topics),
        name="responsibilities",
    )(doc_row, scale, returned, weight, doc_topic, totals)
    return (resp_new.reshape(owners, slots, topics), word_topic, doc_topic)


def solution(mesh):
    return jax.shard_map(
        on_device,
        mesh=mesh,
        in_specs=(P("dp", "vocab"), P("dp", "vocab"), P("dp", "vocab"), P("dp", "vocab", None)),
        out_specs=(P("dp", "vocab", None), P(("dp", "vocab"), None), P("dp", None)),
        check_vma=False,
    )
```

```python
import math

import jax
import jax.numpy as jnp
from jax import lax
from jax.experimental import pallas as pl
from jax.experimental.pallas import tpu as pltpu
from jax.sharding import PartitionSpec as P

VOC_DEV = 2048
DOCS = 64
BF = jnp.bfloat16
F32 = jnp.float32
I32 = jnp.int32
ALPHA = 0.1
BETA = 0.01
LANES = 128
HALF = 64
WORD_AT = 124
CODES = 65535


def code_range(slots, topics):
    most = BETA + 4.0 * slots * (10.2 / (10.2 + (topics - 1) * 0.0985))
    low, high = math.log2(BETA) - 1e-3, math.log2(most) + 1e-3
    step = (high - low) / (CODES - 1)
    return step, low + (CODES // 2) * step


def dot(a, b):
    return jnp.dot(a, b, preferred_element_type=F32)


def split(x):
    high = x.astype(BF)
    return high, (x - high.astype(F32)).astype(BF)


def weight_sums(weight):
    ones = jnp.ones((8, weight.shape[1]), BF)
    return lax.dot_general(ones, weight, (((1,), (1,)), ((), ())), preferred_element_type=F32)


def flat_column(x, slots):
    owners = x.shape[1]
    x = jnp.transpose(x)
    x = jnp.broadcast_to(x[:, None, :], (owners, slots, slots)).reshape(owners * slots, slots)
    row = lax.broadcasted_iota(I32, x.shape, 0) % slots
    lane = lax.broadcasted_iota(I32, x.shape, 1)
    return jnp.sum(jnp.where(row == lane, x, 0.0), axis=1, keepdims=True)


def prepare_kernel(
    word_ref, count_ref, doc_ref, weight_ref, out_ref, rows_ref, words, counts, docs, held, beside, sems
):
    flat, topics = held.shape
    slots = words.shape[0]
    pieces = [slice(i, i + flat // 4) for i in range(0, flat, flat // 4)]
    pairs = [(word_ref, words), (count_ref, counts), (doc_ref, docs)]
    pairs += [(weight_ref.at[at], held.at[at]) for at in pieces]
    loads = [pltpu.make_async_copy(a, b, sems.at[i]) for i, (a, b) in enumerate(pairs)]
    stores = [
        pltpu.make_async_copy(held.at[at], out_ref.at[at, pl.ds(0, topics)], sems.at[7 + i])
        for i, at in enumerate(pieces)
    ]
    stores.append(pltpu.make_async_copy(beside, out_ref.at[:, pl.ds(topics, LANES)], sems.at[11]))
    for load in loads:
        load.start()
    for load in loads[:3]:
        load.wait()
    word = flat_column(words[...].astype(F32), slots)
    count = flat_column(counts[...].astype(F32), slots)
    doc = flat_column(docs[...].astype(F32), slots)
    lane = lax.broadcasted_iota(I32, (flat, LANES), 1)
    rows = jnp.transpose(jnp.where(lane == 0, count, doc))
    for load, store in zip(loads[3:], stores):
        load.wait()
        store.start()
    scale = rows[0:1] / weight_sums(held[...])
    rows_ref[...] = jnp.where(lax.broadcasted_iota(I32, (8, flat), 0) == 0, scale, rows[1:2])
    first, second = split(scale)
    sums = dot(first, held[...]) + dot(second, held[...])
    tile = jnp.concatenate([sums[0:1, HALF * i : HALF * i + HALF] for i in range(slots)], axis=0)
    first, second = split(tile)
    tile = jnp.concatenate([first.astype(F32), second.astype(F32)], axis=1)
    tile = jnp.broadcast_to(tile[None], (flat // slots, slots, LANES)).reshape(flat, LANES)
    scale = jnp.transpose(scale)[:, 0:1]
    first, second = split(scale)
    high = jnp.floor(word * 0.125)
    parts = (high, word - high * 8.0, first.astype(F32), second.astype(F32))
    for i, part in enumerate(parts):
        tile = jnp.where(lane == WORD_AT + i, part, tile)
    beside[...] = tile.astype(BF)
    stores[-1].start()
    for store in stores:
        store.wait()


def doc_kernel(rows_ref, weight_ref, out_ref):
    slots = rows_ref.shape[1]
    ids = lax.broadcasted_iota(I32, (DOCS, slots), 0)
    high, low = split(jnp.where(ids == rows_ref[1:2].astype(I32), rows_ref[0:1], 0.0))
    out_ref[...] = dot(high, weight_ref[...]) + dot(low, weight_ref[...])


def owner_kernel(step, middle, slots, arrived_ref, docs_ref, out_ref, rows_ref, docs_out_ref, code_ref, sems):
    flat, topics = code_ref.shape
    beside = arrived_ref[:, topics:].astype(F32)
    across = jnp.transpose(beside)
    rows_ref[...] = across[LANES - 8 :]
    word_column = beside[:, WORD_AT : WORD_AT + 1] * 8.0 + beside[:, WORD_AT + 1 : WORD_AT + 2]
    word_row = across[WORD_AT : WORD_AT + 1] * 8.0 + across[WORD_AT + 1 : WORD_AT + 2]
    rows = lax.broadcasted_iota(I32, (flat, flat), 0)
    columns = lax.broadcasted_iota(I32, (flat, flat), 1)
    others = (word_column == word_row) & (rows != columns)
    high = jnp.where(others, across[WORD_AT + 2 : WORD_AT + 3], 0.0).astype(BF)
    low = jnp.where(others, across[WORD_AT + 3 : WORD_AT + 4], 0.0).astype(BF)
    width = 256
    copies = []
    for i in range(topics // width):
        at = slice(i * width, i * width + width)
        weight = arrived_ref[:, at]
        value = dot(high, weight) + dot(low, weight) + BETA
        code = (jnp.log2(value) - middle) * (1.0 / step)
        code_ref[:, at] = jnp.round(code).astype(I32).astype(jnp.int16)
        copies.append(pltpu.make_async_copy(code_ref.at[:, at], out_ref.at[:, at], sems.at[i]))
        copies[-1].start()
    sums = jnp.sum(beside.reshape(flat // slots, slots, LANES), axis=0)
    lane = lax.broadcasted_iota(I32, (slots, LANES), 1)
    sums = jnp.where(lane >= WORD_AT, 0.0, sums)
    sums = sums + pltpu.roll(sums, HALF, 1)
    docs_out_ref[:, :topics] = docs_ref[...]
    docs_out_ref[:, topics:] = jnp.where(lane[:8] < HALF, sums[:8], sums[8:])
    for copy in copies:
        copy.wait()


def word_kernel(rows_ref, weight_ref, out_ref):
    rows, slots = out_ref.shape[0], rows_ref.shape[1]
    at = WORD_AT - (LANES - 8)
    word = (rows_ref[at : at + 1] * 8.0 + rows_ref[at + 1 : at + 2]).astype(I32)
    same = lax.broadcasted_iota(I32, (rows, slots), 0) + pl.program_id(0) * rows == word
    high = jnp.where(same, rows_ref[at + 2 : at + 3], 0.0).astype(BF)
    low = jnp.where(same, rows_ref[at + 3 : at + 4], 0.0).astype(BF)
    weight = weight_ref[:, : out_ref.shape[1]]
    out_ref[...] = dot(high, weight) + dot(low, weight)


def factor_kernel(beta_all, rows_ref, weight_ref, docs_ref, out_ref):
    slots, topics = weight_ref.shape
    scale = jnp.transpose(rows_ref[...])[:, 0:1]
    ids = lax.broadcasted_iota(I32, (DOCS, slots), 0)
    picked = jnp.transpose((ids == rows_ref[1:2].astype(I32)).astype(F32)).astype(BF)
    doc_high, doc_low = split(docs_ref[:, :topics])
    doc_rows = dot(picked, doc_high) + dot(picked, doc_low) + ALPHA
    parts = docs_ref[0:8, topics:]
    for i in range(1, DOCS // 8):
        parts = parts + docs_ref[8 * i : 8 * i + 8, topics:]
    pieces = [parts[i : i + 1, j : j + HALF] for j in (0, HALF) for i in range(8)]
    totals = jnp.concatenate(pieces, axis=1) + beta_all
    share = scale * weight_ref[...].astype(F32)
    out_ref[...] = (doc_rows - share) / (totals - share)


def new_kernel(step, code_ref, factor_ref, out_ref, codes, held, sems):
    flat = codes.shape[0]
    number = sems.shape[0] // 2
    pieces = [slice(i, i + flat // number) for i in range(0, flat, flat // number)]
    loads = [pltpu.make_async_copy(code_ref.at[at], codes.at[at], sems.at[i]) for i, at in enumerate(pieces)]
    stores = [
        pltpu.make_async_copy(held.at[at], out_ref.at[at], sems.at[number + i]) for i, at in enumerate(pieces)
    ]
    for load in loads:
        load.start()
    for at, load, store in zip(pieces, loads, stores):
        load.wait()
        raw = jnp.exp2(codes[at].astype(I32).astype(F32) * step) * factor_ref[at]
        norm = 1.0 / jnp.sum(raw, axis=-1, keepdims=True)
        held[at] = (raw * norm).astype(BF)
        store.start()
    for store in stores:
        store.wait()


def cost(flops, nbytes):
    return pl.CostEstimate(flops=flops, bytes_accessed=nbytes, transcendentals=0)


def swap(x, dy, dc):
    return lax.ppermute(x, "vocab", [(i, ((i // 2 + dy) % 4) * 2 + (i + dc) % 2) for i in range(8)])


def docs_scatter(x, topics):
    me = lax.axis_index("vocab")
    y, core = me // 2, me % 2
    x = x.reshape(4, 2, DOCS // 8, topics)
    mine = lax.dynamic_index_in_dim(x, core, 1, keepdims=False)
    mine = mine + swap(lax.dynamic_index_in_dim(x, 1 - core, 1, keepdims=False), 0, 1)
    total = lax.dynamic_index_in_dim(mine, y, 0, keepdims=False)
    for dy in range(1, 4):
        total = total + swap(lax.dynamic_index_in_dim(mine, (y + dy) % 4, 0, keepdims=False), dy, 0)
    return total


def on_device(slot_word, slot_doc, slot_count, resp_weight):
    owners, slots, topics = resp_weight.shape
    flat, wide = owners * slots, topics + LANES
    vocab_total = VOC_DEV * lax.axis_size("dp") * lax.axis_size("vocab")
    step, middle = code_range(flat, topics)
    params = pltpu.CompilerParams(vmem_limit_bytes=48 * 1024 * 1024)
    vmem, hbm = pl.BlockSpec(memory_space=pltpu.VMEM), pl.BlockSpec(memory_space=pltpu.HBM)
    row_shape = jax.ShapeDtypeStruct((8, flat), F32)

    weight = resp_weight.reshape(flat, topics)
    sent, local_rows = pl.pallas_call(
        prepare_kernel,
        out_shape=(jax.ShapeDtypeStruct((flat, wide), BF), row_shape),
        in_specs=[hbm, hbm, hbm, hbm],
        out_specs=(hbm, vmem),
        scratch_shapes=[pltpu.VMEM((slots, owners), I32)] * 3
        + [
            pltpu.VMEM((flat, topics), BF),
            pltpu.VMEM((flat, LANES), BF),
            pltpu.SemaphoreType.DMA((12,)),
        ],
        compiler_params=pltpu.CompilerParams(vmem_limit_bytes=60 * 1024 * 1024),
        cost_estimate=cost(4 * 8 * flat * topics, 4 * flat * topics),
        name="prepare",
    )(slot_word.T, slot_count.T, slot_doc.T, weight)
    arrived = lax.all_to_all(
        sent.reshape(owners, slots, wide), "dp", split_axis=0, concat_axis=0, tiled=True
    ).reshape(flat, wide)

    doc_partial = pl.pallas_call(
        doc_kernel,
        out_shape=jax.ShapeDtypeStruct((DOCS, topics), F32),
        compiler_params=params,
        cost_estimate=cost(2 * 2 * DOCS * flat * topics, 2 * flat * topics),
        name="doc_counts",
    )(local_rows, weight)
    docs_own = docs_scatter(doc_partial, topics)

    code, owned_rows, docs_out = pl.pallas_call(
        lambda *refs: owner_kernel(step, middle, slots, *refs),
        out_shape=(
            jax.ShapeDtypeStruct((flat, topics), jnp.int16),
            row_shape,
            jax.ShapeDtypeStruct((DOCS // 8, wide), F32),
        ),
        in_specs=[vmem, vmem],
        out_specs=(hbm, vmem, vmem),
        scratch_shapes=[pltpu.VMEM((flat, topics), jnp.int16), pltpu.SemaphoreType.DMA((4,))],
        compiler_params=params,
        cost_estimate=cost(2 * 2 * flat * flat * topics, 4 * flat * topics),
        name="word_rows",
    )(arrived, docs_own)
    returned = lax.all_to_all(
        code.reshape(owners, slots, topics), "dp", split_axis=0, concat_axis=0, tiled=True
    ).reshape(flat, topics)
    docs_all = lax.all_gather(docs_out, "vocab", axis=0, tiled=True)

    block = 256
    word_topic = pl.pallas_call(
        word_kernel,
        out_shape=jax.ShapeDtypeStruct((VOC_DEV, topics), F32),
        grid=(VOC_DEV // block,),
        in_specs=[pl.BlockSpec((8, flat), lambda i: (0, 0)), pl.BlockSpec((flat, wide), lambda i: (0, 0))],
        out_specs=pl.BlockSpec((block, topics), lambda i: (i, 0)),
        compiler_params=params,
        cost_estimate=cost(2 * 2 * VOC_DEV * flat * topics, 4 * VOC_DEV * topics),
        name="word_counts",
    )(owned_rows, arrived)

    rows = min(128, flat)
    across = pl.BlockSpec((rows, topics), lambda i: (i, 0))
    factors = pl.pallas_call(
        lambda *refs: factor_kernel(BETA * vocab_total, *refs),
        out_shape=jax.ShapeDtypeStruct((flat, topics), F32),
        grid=(flat // rows,),
        in_specs=[
            pl.BlockSpec((8, rows), lambda i: (0, i)),
            across,
            pl.BlockSpec(docs_all.shape, lambda i: (0, 0)),
        ],
        out_specs=across,
        compiler_params=params,
        cost_estimate=cost(2 * 2 * DOCS * flat * topics, 6 * flat * topics),
        name="factors",
    )(local_rows, weight, docs_all)
    resp_new = pl.pallas_call(
        lambda *refs: new_kernel(step, *refs),
        out_shape=jax.ShapeDtypeStruct((flat, topics), BF),
        in_specs=[hbm, vmem],
        out_specs=hbm,
        scratch_shapes=[
            pltpu.VMEM((flat, topics), jnp.int16),
            pltpu.VMEM((flat, topics), BF),
            pltpu.SemaphoreType.DMA((8,)),
        ],
        compiler_params=params,
        cost_estimate=cost(8 * flat * topics, 8 * flat * topics),
        name="responsibilities",
    )(returned, factors)
    return (resp_new.reshape(owners, slots, topics), word_topic, docs_all[:, :topics])


def solution(mesh):
    return jax.shard_map(
        on_device,
        mesh=mesh,
        in_specs=(P("dp", "vocab"), P("dp", "vocab"), P("dp", "vocab"), P("dp", "vocab", None)),
        out_specs=(P("dp", "vocab", None), P(("dp", "vocab"), None), P("dp", None)),
        check_vma=False,
    )
```

```python
import math

import jax
import jax.numpy as jnp
from jax import lax
from jax.experimental import pallas as pl
from jax.experimental.pallas import tpu as pltpu
from jax.sharding import PartitionSpec as P

VOC_DEV = 2048
DOCS = 64
BF = jnp.bfloat16
F32 = jnp.float32
I32 = jnp.int32
ALPHA = 0.1
BETA = 0.01
LANES = 128
HALF = 64
WORD_AT = 124
CODES = 65535


def code_range(slots, topics):
    most = BETA + 4.0 * slots * (10.2 / (10.2 + (topics - 1) * 0.0985))
    low, high = math.log2(BETA) - 1e-3, math.log2(most) + 1e-3
    step = (high - low) / (CODES - 1)
    return step, low + (CODES // 2) * step


def dot(a, b):
    return jnp.dot(a, b, preferred_element_type=F32)


def split(x):
    high = x.astype(BF)
    return high, (x - high.astype(F32)).astype(BF)


def weight_sums(weight):
    ones = jnp.ones((8, weight.shape[1]), BF)
    return lax.dot_general(ones, weight, (((1,), (1,)), ((), ())), preferred_element_type=F32)


def flat_column(x, slots):
    owners = x.shape[1]
    x = jnp.transpose(x)
    x = jnp.broadcast_to(x[:, None, :], (owners, slots, slots)).reshape(owners * slots, slots)
    row = lax.broadcasted_iota(I32, x.shape, 0) % slots
    lane = lax.broadcasted_iota(I32, x.shape, 1)
    return jnp.sum(jnp.where(row == lane, x, 0.0), axis=1, keepdims=True)


def prepare_kernel(word_ref, count_ref, weight_ref, out_ref, words, counts, held, beside, sems):
    flat, topics = held.shape
    slots = words.shape[0]
    pairs = ((word_ref, words), (count_ref, counts), (weight_ref, held))
    loads = [pltpu.make_async_copy(a, b, sems.at[i]) for i, (a, b) in enumerate(pairs)]
    through = pltpu.make_async_copy(held, out_ref.at[:, pl.ds(0, topics)], sems.at[3])
    store = pltpu.make_async_copy(beside, out_ref.at[:, pl.ds(topics, LANES)], sems.at[4])
    for load in loads:
        load.start()
    for load in loads[:2]:
        load.wait()
    meta = flat_column((words[...] * 8 + counts[...]).astype(F32), slots)
    word = jnp.floor(meta * 0.125)
    count = meta - word * 8.0
    ones = jnp.ones((topics, LANES), BF)
    loads[2].wait()
    through.start()
    scale = count / dot(held[...], ones)
    sums = jnp.sum(scale[:, 0:1] * held[...].astype(F32), axis=0, keepdims=True)
    tile = jnp.concatenate([sums[:, HALF * i : HALF * i + HALF] for i in range(slots)], axis=0)
    first, second = split(tile)
    tile = jnp.concatenate([first.astype(F32), second.astype(F32)], axis=1)
    tile = jnp.broadcast_to(tile[None], (flat // slots, slots, LANES)).reshape(flat, LANES)
    first, second = split(scale)
    high = jnp.floor(word * 0.125)
    lane = lax.broadcasted_iota(I32, (flat, LANES), 1)
    parts = (high, word - high * 8.0, first.astype(F32), second.astype(F32))
    for i, part in enumerate(parts):
        tile = jnp.where(lane == WORD_AT + i, part, tile)
    beside[...] = tile.astype(BF)
    store.start()
    through.wait()
    store.wait()


def doc_kernel(count_ref, doc_ref, weight_ref, out_ref, rows_ref):
    slots = count_ref.shape[0]
    flat = weight_ref.shape[0]
    count = flat_column(count_ref[...].astype(F32), slots)
    doc = flat_column(doc_ref[...].astype(F32), slots)
    lane = lax.broadcasted_iota(I32, (flat, LANES), 1)
    rows = jnp.transpose(jnp.where(lane == 0, count, doc))
    scale = rows[0:1] / weight_sums(weight_ref[...])
    rows_ref[...] = jnp.where(lax.broadcasted_iota(I32, (8, flat), 0) == 0, scale, rows[1:2])
    ids = lax.broadcasted_iota(I32, (DOCS, flat), 0)
    high, low = split(jnp.where(ids == rows[1:2].astype(I32), scale[0:1], 0.0))
    out_ref[...] = dot(high, weight_ref[...]) + dot(low, weight_ref[...])


def owner_kernel(step, middle, slots, arrived_ref, docs_ref, out_ref, rows_ref, sums_ref, code_ref, sems):
    flat, topics = code_ref.shape
    beside = arrived_ref[:, topics:].astype(F32)
    across = jnp.transpose(beside)
    rows_ref[...] = across[LANES - 8 :]
    word_column = beside[:, WORD_AT : WORD_AT + 1] * 8.0 + beside[:, WORD_AT + 1 : WORD_AT + 2]
    word_row = across[WORD_AT : WORD_AT + 1] * 8.0 + across[WORD_AT + 1 : WORD_AT + 2]
    rows = lax.broadcasted_iota(I32, (flat, flat), 0)
    columns = lax.broadcasted_iota(I32, (flat, flat), 1)
    others = (word_column == word_row) & (rows != columns)
    high = jnp.where(others, across[WORD_AT + 2 : WORD_AT + 3], 0.0).astype(BF)
    low = jnp.where(others, across[WORD_AT + 3 : WORD_AT + 4], 0.0).astype(BF)
    both = jnp.concatenate([high, low], axis=0)
    width = 256
    copies = []
    for i in range(topics // width):
        at = slice(i * width, i * width + width)
        weight = arrived_ref[:, at]
        value = dot(both, weight)
        value = value[:flat] + value[flat:] + BETA
        code = (jnp.log2(value) - middle) * (1.0 / step)
        code_ref[:, at] = jnp.round(code).astype(I32).astype(jnp.int16)
        copies.append(pltpu.make_async_copy(code_ref.at[:, at], out_ref.at[:, at], sems.at[i]))
        copies[-1].start()
    sums = jnp.sum(beside.reshape(flat // slots, slots, LANES), axis=0)
    lane = lax.broadcasted_iota(I32, (slots, LANES), 1)
    sums = jnp.where(lane >= WORD_AT, 0.0, sums)
    sums = sums + pltpu.roll(sums, HALF, 1)
    sums_ref[...] = jnp.where(lane[:8] < HALF, sums[:8], sums[8:])
    for copy in copies:
        copy.wait()


def word_kernel(rows_ref, weight_ref, factor_ref, out_ref):
    rows, slots = out_ref.shape[0], rows_ref.shape[1]
    at = WORD_AT - (LANES - 8)
    word = (rows_ref[at : at + 1] * 8.0 + rows_ref[at + 1 : at + 2]).astype(I32)
    same = lax.broadcasted_iota(I32, (rows, slots), 0) + pl.program_id(0) * rows == word
    high = jnp.where(same, rows_ref[at + 2 : at + 3], 0.0).astype(BF)
    low = jnp.where(same, rows_ref[at + 3 : at + 4], 0.0).astype(BF)
    weight = weight_ref[:, : out_ref.shape[1]]
    out_ref[...] = dot(high, weight) + dot(low, weight)


def factor_kernel(beta_all, rows_ref, weight_ref, docs_ref, sums_ref, out_ref):
    slots, topics = weight_ref.shape
    scale = jnp.transpose(rows_ref[...])[:, 0:1]
    ids = lax.broadcasted_iota(I32, (DOCS, slots), 0)
    picked = jnp.transpose((ids == rows_ref[1:2].astype(I32)).astype(F32)).astype(BF)
    doc_high, doc_low = split(docs_ref[:, :topics])
    doc_rows = dot(picked, doc_high) + dot(picked, doc_low) + ALPHA
    pieces = [sums_ref[i : i + 1, j : j + HALF] for j in (0, HALF) for i in range(8)]
    totals = jnp.concatenate(pieces, axis=1) + beta_all
    share = scale * weight_ref[...].astype(F32)
    out_ref[...] = (doc_rows - share) / (totals - share)


def new_kernel(step, code_ref, factor_ref, out_ref):
    raw = jnp.exp2(code_ref[...].astype(I32).astype(F32) * step) * factor_ref[...]
    norm = 1.0 / jnp.sum(raw, axis=-1, keepdims=True)
    out_ref[...] = (raw * norm).astype(BF)


def cost(flops, nbytes):
    return pl.CostEstimate(flops=flops, bytes_accessed=nbytes, transcendentals=0)


def swap(x, dy, dc):
    return lax.ppermute(x, "vocab", [(i, ((i // 2 + dy) % 4) * 2 + (i + dc) % 2) for i in range(8)])


def docs_scatter(x, topics):
    me = lax.axis_index("vocab")
    y, core = me // 2, me % 2
    x = x.reshape(4, 2, DOCS // 8, topics)
    mine = lax.dynamic_index_in_dim(x, core, 1, keepdims=False)
    mine = mine + swap(lax.dynamic_index_in_dim(x, 1 - core, 1, keepdims=False), 0, 1)
    total = lax.dynamic_index_in_dim(mine, y, 0, keepdims=False)
    for dy in range(1, 4):
        total = total + swap(lax.dynamic_index_in_dim(mine, (y + dy) % 4, 0, keepdims=False), dy, 0)
    return total


def on_device(slot_word, slot_doc, slot_count, resp_weight):
    owners, slots, topics = resp_weight.shape
    flat, wide = owners * slots, topics + LANES
    vocab_total = VOC_DEV * lax.axis_size("dp") * lax.axis_size("vocab")
    step, middle = code_range(flat, topics)
    params = pltpu.CompilerParams(vmem_limit_bytes=16 * 1024 * 1024)
    vmem, hbm = pl.BlockSpec(memory_space=pltpu.VMEM), pl.BlockSpec(memory_space=pltpu.HBM)
    row_shape = jax.ShapeDtypeStruct((8, flat), F32)

    weight = resp_weight.reshape(flat, topics)
    sent = pl.pallas_call(
        prepare_kernel,
        out_shape=jax.ShapeDtypeStruct((flat, wide), BF),
        in_specs=[hbm, hbm, hbm],
        out_specs=hbm,
        scratch_shapes=[pltpu.VMEM((slots, owners), I32)] * 2
        + [
            pltpu.VMEM((flat, topics), BF),
            pltpu.VMEM((flat, LANES), BF),
            pltpu.SemaphoreType.DMA((5,)),
        ],
        compiler_params=pltpu.CompilerParams(vmem_limit_bytes=60 * 1024 * 1024),
        cost_estimate=cost(4 * 8 * flat * topics, 4 * flat * topics),
        name="prepare",
    )(slot_word.T, slot_count.T, weight)
    arrived = lax.all_to_all(
        sent.reshape(owners, slots, wide), "dp", split_axis=0, concat_axis=0, tiled=True
    ).reshape(flat, wide)

    doc_partial, local_rows = pl.pallas_call(
        doc_kernel,
        out_shape=(jax.ShapeDtypeStruct((DOCS, topics), F32), row_shape),
        compiler_params=params,
        cost_estimate=cost(2 * 2 * DOCS * flat * topics, 2 * flat * topics),
        name="doc_counts",
    )(slot_count.T, slot_doc.T, weight)
    docs_own = docs_scatter(doc_partial, topics)
    docs_own = jnp.concatenate([docs_own, jnp.zeros((DOCS // 8, LANES), F32)], axis=1)
    docs_all = lax.all_gather(docs_own, "vocab", axis=0, tiled=True)

    code, owned_rows, group_sums = pl.pallas_call(
        lambda *refs: owner_kernel(step, middle, slots, *refs),
        out_shape=(
            jax.ShapeDtypeStruct((flat, topics), jnp.int16),
            row_shape,
            jax.ShapeDtypeStruct((8, LANES), F32),
        ),
        in_specs=[vmem, hbm],
        out_specs=(hbm, vmem, vmem),
        scratch_shapes=[pltpu.VMEM((flat, topics), jnp.int16), pltpu.SemaphoreType.DMA((4,))],
        compiler_params=params,
        cost_estimate=cost(2 * 2 * flat * flat * topics, 4 * flat * topics),
        name="word_rows",
    )(arrived, docs_all)
    returned = lax.all_to_all(
        code.reshape(owners, slots, topics), "dp", split_axis=0, concat_axis=0, tiled=True
    ).reshape(flat, topics)
    totals = group_sums + swap(group_sums, 0, 1)
    totals = totals + swap(totals, 1, 0) + swap(totals, 2, 0) + swap(totals, 3, 0)

    rows = min(128, flat)
    across = pl.BlockSpec((rows, topics), lambda i: (i, 0))
    factors = pl.pallas_call(
        lambda *refs: factor_kernel(BETA * vocab_total, *refs),
        out_shape=jax.ShapeDtypeStruct((flat, topics), F32),
        grid=(flat // rows,),
        in_specs=[
            pl.BlockSpec((8, rows), lambda i: (0, i)),
            across,
            pl.BlockSpec((DOCS, wide), lambda i: (0, 0)),
            pl.BlockSpec((8, LANES), lambda i: (0, 0)),
        ],
        out_specs=across,
        compiler_params=pltpu.CompilerParams(vmem_limit_bytes=60 * 1024 * 1024),
        cost_estimate=cost(2 * 2 * DOCS * flat * topics, 6 * flat * topics),
        name="factors",
    )(local_rows, weight, docs_all, totals)
    block = 256
    word_topic = pl.pallas_call(
        word_kernel,
        out_shape=jax.ShapeDtypeStruct((VOC_DEV, topics), F32),
        grid=(VOC_DEV // block,),
        in_specs=[pl.BlockSpec((8, flat), lambda i: (0, 0)), pl.BlockSpec((flat, wide), lambda i: (0, 0)), hbm],
        out_specs=pl.BlockSpec((block, topics), lambda i: (i, 0)),
        compiler_params=pltpu.CompilerParams(vmem_limit_bytes=60 * 1024 * 1024),
        cost_estimate=cost(2 * 2 * VOC_DEV * flat * topics, 4 * VOC_DEV * topics),
        name="word_counts",
    )(owned_rows, arrived, factors)

    half = pl.BlockSpec((flat // 2, topics), lambda i: (i, 0))
    resp_new = pl.pallas_call(
        lambda *refs: new_kernel(step, *refs),
        out_shape=jax.ShapeDtypeStruct((flat, topics), BF),
        grid=(2,),
        in_specs=[half, half],
        out_specs=half,
        compiler_params=params,
        cost_estimate=cost(8 * flat * topics, 8 * flat * topics),
        name="responsibilities",
    )(returned, factors)
    return (resp_new.reshape(owners, slots, topics), word_topic, docs_all[:, :topics])


def solution(mesh):
    return jax.shard_map(
        on_device,
        mesh=mesh,
        in_specs=(P("dp", "vocab"), P("dp", "vocab"), P("dp", "vocab"), P("dp", "vocab", None)),
        out_specs=(P("dp", "vocab", None), P(("dp", "vocab"), None), P("dp", None)),
        check_vma=False,
    )
```

```python
import math

import jax
import jax.numpy as jnp
from jax import lax
from jax.experimental import pallas as pl
from jax.experimental.pallas import tpu as pltpu
from jax.sharding import PartitionSpec as P

VOC_DEV = 2048
DOCS = 64
BF = jnp.bfloat16
F32 = jnp.float32
I32 = jnp.int32
ALPHA = 0.1
BETA = 0.01
LANES = 128
HALF = 64
WORD_AT = 124
CODES = 65535


def code_range(slots, topics):
    most = BETA + 4.0 * slots * (10.2 / (10.2 + (topics - 1) * 0.0985))
    low, high = math.log2(BETA) - 1e-3, math.log2(most) + 1e-3
    step = (high - low) / (CODES - 1)
    return step, low + (CODES // 2) * step


def dot(a, b):
    return jnp.dot(a, b, preferred_element_type=F32)


def split(x):
    high = x.astype(BF)
    return high, (x - high.astype(F32)).astype(BF)


def weight_sums(weight):
    ones = jnp.ones((8, weight.shape[1]), BF)
    return lax.dot_general(ones, weight, (((1,), (1,)), ((), ())), preferred_element_type=F32)


def flat_column(x, slots):
    owners = x.shape[1]
    x = jnp.transpose(x)
    x = jnp.broadcast_to(x[:, None, :], (owners, slots, slots)).reshape(owners * slots, slots)
    row = lax.broadcasted_iota(I32, x.shape, 0) % slots
    lane = lax.broadcasted_iota(I32, x.shape, 1)
    return jnp.sum(jnp.where(row == lane, x, 0.0), axis=1, keepdims=True)


def prepare_kernel(word_ref, count_ref, weight_ref, out_ref, words, counts, held, beside, sems):
    flat, topics = held.shape
    slots = words.shape[0]
    pairs = ((word_ref, words), (count_ref, counts), (weight_ref, held))
    loads = [pltpu.make_async_copy(a, b, sems.at[i]) for i, (a, b) in enumerate(pairs)]
    through = pltpu.make_async_copy(held, out_ref.at[:, pl.ds(0, topics)], sems.at[3])
    store = pltpu.make_async_copy(beside, out_ref.at[:, pl.ds(topics, LANES)], sems.at[4])
    for load in loads:
        load.start()
    for load in loads[:2]:
        load.wait()
    meta = flat_column((words[...] * 8 + counts[...]).astype(F32), slots)
    word = jnp.floor(meta * 0.125)
    count = meta - word * 8.0
    ones = jnp.ones((topics, LANES), BF)
    loads[2].wait()
    through.start()
    scale = count / dot(held[...], ones)
    sums = jnp.sum(scale[:, 0:1] * held[...].astype(F32), axis=0, keepdims=True)
    tile = jnp.concatenate([sums[:, HALF * i : HALF * i + HALF] for i in range(slots)], axis=0)
    first, second = split(tile)
    tile = jnp.concatenate([first.astype(F32), second.astype(F32)], axis=1)
    tile = jnp.broadcast_to(tile[None], (flat // slots, slots, LANES)).reshape(flat, LANES)
    first, second = split(scale)
    high = jnp.floor(word * 0.125)
    lane = lax.broadcasted_iota(I32, (flat, LANES), 1)
    parts = (high, word - high * 8.0, first.astype(F32), second.astype(F32))
    for i, part in enumerate(parts):
        tile = jnp.where(lane == WORD_AT + i, part, tile)
    beside[...] = tile.astype(BF)
    store.start()
    through.wait()
    store.wait()


def doc_kernel(count_ref, doc_ref, weight_ref, out_ref, rows_ref):
    slots = count_ref.shape[0]
    flat = weight_ref.shape[0]
    count = flat_column(count_ref[...].astype(F32), slots)
    doc = flat_column(doc_ref[...].astype(F32), slots)
    lane = lax.broadcasted_iota(I32, (flat, LANES), 1)
    rows = jnp.transpose(jnp.where(lane == 0, count, doc))
    scale = rows[0:1] / weight_sums(weight_ref[...])
    rows_ref[...] = jnp.where(lax.broadcasted_iota(I32, (8, flat), 0) == 0, scale, rows[1:2])
    ids = lax.broadcasted_iota(I32, (DOCS, flat), 0)
    high, low = split(jnp.where(ids == rows[1:2].astype(I32), scale[0:1], 0.0))
    out_ref[...] = dot(high, weight_ref[...]) + dot(low, weight_ref[...])


def owner_kernel(step, middle, slots, arrived_ref, docs_ref, out_ref, sums_ref, code_ref, sems):
    flat, topics = code_ref.shape
    beside = arrived_ref[:, topics:].astype(F32)
    across = jnp.transpose(beside)
    word_column = beside[:, WORD_AT : WORD_AT + 1] * 8.0 + beside[:, WORD_AT + 1 : WORD_AT + 2]
    word_row = across[WORD_AT : WORD_AT + 1] * 8.0 + across[WORD_AT + 1 : WORD_AT + 2]
    rows = lax.broadcasted_iota(I32, (flat, flat), 0)
    columns = lax.broadcasted_iota(I32, (flat, flat), 1)
    others = (word_column == word_row) & (rows != columns)
    high = jnp.where(others, across[WORD_AT + 2 : WORD_AT + 3], 0.0).astype(BF)
    low = jnp.where(others, across[WORD_AT + 3 : WORD_AT + 4], 0.0).astype(BF)
    both = jnp.concatenate([high, low], axis=0)
    width = 256
    copies = []
    for i in range(topics // width):
        at = slice(i * width, i * width + width)
        weight = arrived_ref[:, at]
        value = dot(both, weight)
        value = value[:flat] + value[flat:] + BETA
        code = (jnp.log2(value) - middle) * (1.0 / step)
        code_ref[:, at] = jnp.round(code).astype(I32).astype(jnp.int16)
        copies.append(pltpu.make_async_copy(code_ref.at[:, at], out_ref.at[:, at], sems.at[i]))
        copies[-1].start()
    sums = jnp.sum(beside.reshape(flat // slots, slots, LANES), axis=0)
    lane = lax.broadcasted_iota(I32, (slots, LANES), 1)
    sums = jnp.where(lane >= WORD_AT, 0.0, sums)
    sums = sums + pltpu.roll(sums, HALF, 1)
    sums_ref[...] = jnp.where(lane[:8] < HALF, sums[:8], sums[8:])
    for copy in copies:
        copy.wait()


def word_kernel(arrived_ref, factor_ref, out_ref, across):
    rows, topics = out_ref.shape
    slots = arrived_ref.shape[0]

    @pl.when(pl.program_id(0) == 0)
    def _():
        across[...] = jnp.transpose(arrived_ref[:, topics:].astype(F32))

    word = (across[WORD_AT : WORD_AT + 1] * 8.0 + across[WORD_AT + 1 : WORD_AT + 2]).astype(I32)
    same = lax.broadcasted_iota(I32, (rows, slots), 0) + pl.program_id(0) * rows == word
    high = jnp.where(same, across[WORD_AT + 2 : WORD_AT + 3], 0.0).astype(BF)
    low = jnp.where(same, across[WORD_AT + 3 : WORD_AT + 4], 0.0).astype(BF)
    weight = arrived_ref[:, :topics]
    out_ref[...] = dot(high, weight) + dot(low, weight)


def factor_kernel(beta_all, rows_ref, weight_ref, docs_ref, sums_ref, out_ref):
    slots, topics = weight_ref.shape
    scale = jnp.transpose(rows_ref[...])[:, 0:1]
    ids = lax.broadcasted_iota(I32, (DOCS, slots), 0)
    picked = jnp.transpose((ids == rows_ref[1:2].astype(I32)).astype(F32)).astype(BF)
    doc_high, doc_low = split(docs_ref[:, :topics])
    doc_rows = dot(picked, doc_high) + dot(picked, doc_low) + ALPHA
    pieces = [sums_ref[i : i + 1, j : j + HALF] for j in (0, HALF) for i in range(8)]
    totals = jnp.concatenate(pieces, axis=1) + beta_all
    share = scale * weight_ref[...].astype(F32)
    out_ref[...] = (doc_rows - share) / (totals - share)


def new_kernel(step, code_ref, factor_ref, out_ref):
    raw = jnp.exp2(code_ref[...].astype(I32).astype(F32) * step) * factor_ref[...]
    norm = 1.0 / jnp.sum(raw, axis=-1, keepdims=True)
    out_ref[...] = (raw * norm).astype(BF)


def cost(flops, nbytes):
    return pl.CostEstimate(flops=flops, bytes_accessed=nbytes, transcendentals=0)


def swap(x, dy, dc):
    return lax.ppermute(x, "vocab", [(i, ((i // 2 + dy) % 4) * 2 + (i + dc) % 2) for i in range(8)])


def docs_scatter(x, topics):
    me = lax.axis_index("vocab")
    y, core = me // 2, me % 2
    x = x.reshape(4, 2, DOCS // 8, topics)
    mine = lax.dynamic_index_in_dim(x, core, 1, keepdims=False)
    mine = mine + swap(lax.dynamic_index_in_dim(x, 1 - core, 1, keepdims=False), 0, 1)
    total = lax.dynamic_index_in_dim(mine, y, 0, keepdims=False)
    for dy in range(1, 4):
        total = total + swap(lax.dynamic_index_in_dim(mine, (y + dy) % 4, 0, keepdims=False), dy, 0)
    return total


def on_device(slot_word, slot_doc, slot_count, resp_weight):
    owners, slots, topics = resp_weight.shape
    flat, wide = owners * slots, topics + LANES
    vocab_total = VOC_DEV * lax.axis_size("dp") * lax.axis_size("vocab")
    step, middle = code_range(flat, topics)
    params = pltpu.CompilerParams(vmem_limit_bytes=16 * 1024 * 1024)
    vmem, hbm = pl.BlockSpec(memory_space=pltpu.VMEM), pl.BlockSpec(memory_space=pltpu.HBM)
    row_shape = jax.ShapeDtypeStruct((8, flat), F32)

    weight = resp_weight.reshape(flat, topics)
    sent = pl.pallas_call(
        prepare_kernel,
        out_shape=jax.ShapeDtypeStruct((flat, wide), BF),
        in_specs=[hbm, hbm, hbm],
        out_specs=hbm,
        scratch_shapes=[pltpu.VMEM((slots, owners), I32)] * 2
        + [
            pltpu.VMEM((flat, topics), BF),
            pltpu.VMEM((flat, LANES), BF),
            pltpu.SemaphoreType.DMA((5,)),
        ],
        compiler_params=pltpu.CompilerParams(vmem_limit_bytes=60 * 1024 * 1024),
        cost_estimate=cost(4 * 8 * flat * topics, 4 * flat * topics),
        name="prepare",
    )(slot_word.T, slot_count.T, weight)
    arrived = lax.all_to_all(
        sent.reshape(owners, slots, wide), "dp", split_axis=0, concat_axis=0, tiled=True
    ).reshape(flat, wide)

    doc_partial, local_rows = pl.pallas_call(
        doc_kernel,
        out_shape=(jax.ShapeDtypeStruct((DOCS, topics), F32), row_shape),
        compiler_params=params,
        cost_estimate=cost(2 * 2 * DOCS * flat * topics, 2 * flat * topics),
        name="doc_counts",
    )(slot_count.T, slot_doc.T, weight)
    docs_own = docs_scatter(doc_partial, topics)
    docs_own = jnp.concatenate([docs_own, jnp.zeros((DOCS // 8, LANES), F32)], axis=1)
    docs_all = lax.all_gather(docs_own, "vocab", axis=0, tiled=True)

    code, group_sums = pl.pallas_call(
        lambda *refs: owner_kernel(step, middle, slots, *refs),
        out_shape=(
            jax.ShapeDtypeStruct((flat, topics), jnp.int16),
            jax.ShapeDtypeStruct((8, LANES), F32),
        ),
        in_specs=[vmem, hbm],
        out_specs=(hbm, vmem),
        scratch_shapes=[pltpu.VMEM((flat, topics), jnp.int16), pltpu.SemaphoreType.DMA((4,))],
        compiler_params=params,
        cost_estimate=cost(2 * 2 * flat * flat * topics, 4 * flat * topics),
        name="word_rows",
    )(arrived, docs_all)
    returned = lax.all_to_all(
        code.reshape(owners, slots, topics), "dp", split_axis=0, concat_axis=0, tiled=True
    ).reshape(flat, topics)
    totals = group_sums + swap(group_sums, 0, 1)
    totals = totals + swap(totals, 1, 0) + swap(totals, 2, 0) + swap(totals, 3, 0)

    rows = min(128, flat)
    across = pl.BlockSpec((rows, topics), lambda i: (i, 0))
    factors = pl.pallas_call(
        lambda *refs: factor_kernel(BETA * vocab_total, *refs),
        out_shape=jax.ShapeDtypeStruct((flat, topics), F32),
        grid=(flat // rows,),
        in_specs=[
            pl.BlockSpec((8, rows), lambda i: (0, i)),
            across,
            pl.BlockSpec((DOCS, wide), lambda i: (0, 0)),
            pl.BlockSpec((8, LANES), lambda i: (0, 0)),
        ],
        out_specs=across,
        compiler_params=pltpu.CompilerParams(vmem_limit_bytes=60 * 1024 * 1024),
        cost_estimate=cost(2 * 2 * DOCS * flat * topics, 6 * flat * topics),
        name="factors",
    )(local_rows, weight, docs_all, totals)
    block = 256
    word_topic = pl.pallas_call(
        word_kernel,
        out_shape=jax.ShapeDtypeStruct((VOC_DEV, topics), F32),
        grid=(VOC_DEV // block,),
        in_specs=[pl.BlockSpec((flat, wide), lambda i: (0, 0)), hbm],
        out_specs=pl.BlockSpec((block, topics), lambda i: (i, 0)),
        scratch_shapes=[pltpu.VMEM((LANES, flat), F32)],
        compiler_params=pltpu.CompilerParams(vmem_limit_bytes=60 * 1024 * 1024),
        cost_estimate=cost(2 * 2 * VOC_DEV * flat * topics, 4 * VOC_DEV * topics),
        name="word_counts",
    )(arrived, factors)

    half = pl.BlockSpec((flat // 2, topics), lambda i: (i, 0))
    resp_new = pl.pallas_call(
        lambda *refs: new_kernel(step, *refs),
        out_shape=jax.ShapeDtypeStruct((flat, topics), BF),
        grid=(2,),
        in_specs=[half, half],
        out_specs=half,
        compiler_params=params,
        cost_estimate=cost(8 * flat * topics, 8 * flat * topics),
        name="responsibilities",
    )(returned, factors)
    return (resp_new.reshape(owners, slots, topics), word_topic, docs_all[:, :topics])


def solution(mesh):
    return jax.shard_map(
        on_device,
        mesh=mesh,
        in_specs=(P("dp", "vocab"), P("dp", "vocab"), P("dp", "vocab"), P("dp", "vocab", None)),
        out_specs=(P("dp", "vocab", None), P(("dp", "vocab"), None), P("dp", None)),
        check_vma=False,
    )
```

```python
import math

import jax
import jax.numpy as jnp
from jax import lax
from jax.experimental import pallas as pl
from jax.experimental.pallas import tpu as pltpu
from jax.sharding import PartitionSpec as P

VOC_DEV = 2048
DOCS = 64
BF = jnp.bfloat16
F32 = jnp.float32
I32 = jnp.int32
ALPHA = 0.1
BETA = 0.01
LANES = 128
HALF = 64
WORD_AT = 124
CODES = 65535


def code_range(slots, topics):
    most = BETA + 4.0 * slots * (10.2 / (10.2 + (topics - 1) * 0.0985))
    low, high = math.log2(BETA) - 1e-3, math.log2(most) + 1e-3
    step = (high - low) / (CODES - 1)
    return step, low + (CODES // 2) * step


def dot(a, b):
    return jnp.dot(a, b, preferred_element_type=F32)


def split(x):
    high = x.astype(BF)
    return high, (x - high.astype(F32)).astype(BF)


def weight_sums(weight):
    ones = jnp.ones((8, weight.shape[1]), BF)
    return lax.dot_general(ones, weight, (((1,), (1,)), ((), ())), preferred_element_type=F32)


def flat_column(x, slots):
    owners = x.shape[1]
    x = jnp.transpose(x)
    x = jnp.broadcast_to(x[:, None, :], (owners, slots, slots)).reshape(owners * slots, slots)
    row = lax.broadcasted_iota(I32, x.shape, 0) % slots
    lane = lax.broadcasted_iota(I32, x.shape, 1)
    return jnp.sum(jnp.where(row == lane, x, 0.0), axis=1, keepdims=True)


def prepare_kernel(word_ref, count_ref, weight_ref, out_ref, words, counts, held, beside, sems):
    flat, topics = held.shape
    slots = words.shape[0]
    pairs = ((word_ref, words), (count_ref, counts), (weight_ref, held))
    loads = [pltpu.make_async_copy(a, b, sems.at[i]) for i, (a, b) in enumerate(pairs)]
    through = pltpu.make_async_copy(held, out_ref.at[:, pl.ds(0, topics)], sems.at[3])
    store = pltpu.make_async_copy(beside, out_ref.at[:, pl.ds(topics, LANES)], sems.at[4])
    for load in loads:
        load.start()
    for load in loads[:2]:
        load.wait()
    meta = flat_column((words[...] * 8 + counts[...]).astype(F32), slots)
    word = jnp.floor(meta * 0.125)
    count = meta - word * 8.0
    ones = jnp.ones((topics, LANES), BF)
    loads[2].wait()
    through.start()
    scale = count / dot(held[...], ones)
    sums = jnp.sum(scale[:, 0:1] * held[...].astype(F32), axis=0, keepdims=True)
    tile = jnp.concatenate([sums[:, HALF * i : HALF * i + HALF] for i in range(slots)], axis=0)
    first, second = split(tile)
    tile = jnp.concatenate([first.astype(F32), second.astype(F32)], axis=1)
    tile = jnp.broadcast_to(tile[None], (flat // slots, slots, LANES)).reshape(flat, LANES)
    first, second = split(scale)
    high = jnp.floor(word * 0.125)
    lane = lax.broadcasted_iota(I32, (flat, LANES), 1)
    parts = (high, word - high * 8.0, first.astype(F32), second.astype(F32))
    for i, part in enumerate(parts):
        tile = jnp.where(lane == WORD_AT + i, part, tile)
    beside[...] = tile.astype(BF)
    store.start()
    through.wait()
    store.wait()


def doc_kernel(count_ref, doc_ref, weight_ref, out_ref, rows_ref):
    slots = count_ref.shape[0]
    flat = weight_ref.shape[0]
    count = flat_column(count_ref[...].astype(F32), slots)
    doc = flat_column(doc_ref[...].astype(F32), slots)
    lane = lax.broadcasted_iota(I32, (flat, LANES), 1)
    rows = jnp.transpose(jnp.where(lane == 0, count, doc))
    scale = rows[0:1] / weight_sums(weight_ref[...])
    rows_ref[...] = jnp.where(lax.broadcasted_iota(I32, (8, flat), 0) == 0, scale, rows[1:2])
    ids = lax.broadcasted_iota(I32, (DOCS, flat), 0)
    high, low = split(jnp.where(ids == rows[1:2].astype(I32), scale[0:1], 0.0))
    out_ref[...] = dot(high, weight_ref[...]) + dot(low, weight_ref[...])


def owner_kernel(step, middle, slots, arrived_ref, docs_ref, out_ref, sums_ref, code_ref, sems):
    flat, topics = code_ref.shape
    beside = arrived_ref[:, topics:].astype(F32)
    across = jnp.transpose(beside)
    word_column = beside[:, WORD_AT : WORD_AT + 1] * 8.0 + beside[:, WORD_AT + 1 : WORD_AT + 2]
    word_row = across[WORD_AT : WORD_AT + 1] * 8.0 + across[WORD_AT + 1 : WORD_AT + 2]
    rows = lax.broadcasted_iota(I32, (flat, flat), 0)
    columns = lax.broadcasted_iota(I32, (flat, flat), 1)
    others = (word_column == word_row) & (rows != columns)
    high = jnp.where(others, across[WORD_AT + 2 : WORD_AT + 3], 0.0).astype(BF)
    low = jnp.where(others, across[WORD_AT + 3 : WORD_AT + 4], 0.0).astype(BF)
    both = jnp.concatenate([high, low], axis=0)
    width = 256
    copies = []
    for i in range(topics // width):
        at = slice(i * width, i * width + width)
        weight = arrived_ref[:, at]
        value = dot(both, weight)
        value = value[:flat] + value[flat:] + BETA
        code = (jnp.log2(value) - middle) * (1.0 / step)
        code_ref[:, at] = jnp.round(code).astype(I32).astype(jnp.int16)
        copies.append(pltpu.make_async_copy(code_ref.at[:, at], out_ref.at[:, at], sems.at[i]))
        copies[-1].start()
    sums = jnp.sum(beside.reshape(flat // slots, slots, LANES), axis=0)
    lane = lax.broadcasted_iota(I32, (slots, LANES), 1)
    sums = jnp.where(lane >= WORD_AT, 0.0, sums)
    sums = sums + pltpu.roll(sums, HALF, 1)
    sums_ref[...] = jnp.where(lane[:8] < HALF, sums[:8], sums[8:])
    for copy in copies:
        copy.wait()


def word_kernel(arrived_ref, factor_ref, out_ref, across):
    rows, topics = out_ref.shape
    slots = arrived_ref.shape[0]

    @pl.when(pl.program_id(0) == 0)
    def _():
        across[...] = jnp.transpose(arrived_ref[:, topics:].astype(F32))

    word = (across[WORD_AT : WORD_AT + 1] * 8.0 + across[WORD_AT + 1 : WORD_AT + 2]).astype(I32)
    same = lax.broadcasted_iota(I32, (rows, slots), 0) + pl.program_id(0) * rows == word
    high = jnp.where(same, across[WORD_AT + 2 : WORD_AT + 3], 0.0).astype(BF)
    low = jnp.where(same, across[WORD_AT + 3 : WORD_AT + 4], 0.0).astype(BF)
    weight = arrived_ref[:, :topics]
    out_ref[...] = dot(high, weight) + dot(low, weight)


def factor_kernel(beta_all, rows_ref, weight_ref, docs_ref, sums_ref, out_ref):
    slots, topics = weight_ref.shape
    scale = jnp.transpose(rows_ref[...])[:, 0:1]
    ids = lax.broadcasted_iota(I32, (DOCS, slots), 0)
    picked = jnp.transpose((ids == rows_ref[1:2].astype(I32)).astype(F32)).astype(BF)
    doc_high, doc_low = split(docs_ref[:, :topics])
    doc_rows = dot(picked, doc_high) + dot(picked, doc_low) + ALPHA
    pieces = [sums_ref[i : i + 1, j : j + HALF] for j in (0, HALF) for i in range(8)]
    totals = jnp.concatenate(pieces, axis=1) + beta_all
    share = scale * weight_ref[...].astype(F32)
    out_ref[...] = (doc_rows - share) / (totals - share)


def new_kernel(step, code_ref, factor_ref, out_ref):
    raw = jnp.exp2(code_ref[...].astype(I32).astype(F32) * step) * factor_ref[...]
    norm = 1.0 / jnp.sum(raw, axis=-1, keepdims=True)
    out_ref[...] = (raw * norm).astype(BF)


def cost(flops, nbytes):
    return pl.CostEstimate(flops=flops, bytes_accessed=nbytes, transcendentals=0)


def swap(x, dy, dc):
    return lax.ppermute(x, "vocab", [(i, ((i // 2 + dy) % 4) * 2 + (i + dc) % 2) for i in range(8)])


def docs_scatter(x, topics):
    me = lax.axis_index("vocab")
    y, core = me // 2, me % 2
    x = x.reshape(4, 2, DOCS // 8, topics)
    mine = lax.dynamic_index_in_dim(x, core, 1, keepdims=False)
    mine = mine + swap(lax.dynamic_index_in_dim(x, 1 - core, 1, keepdims=False), 0, 1)
    total = lax.dynamic_index_in_dim(mine, y, 0, keepdims=False)
    for dy in range(1, 4):
        total = total + swap(lax.dynamic_index_in_dim(mine, (y + dy) % 4, 0, keepdims=False), dy, 0)
    return total


def on_device(slot_word, slot_doc, slot_count, resp_weight):
    owners, slots, topics = resp_weight.shape
    flat, wide = owners * slots, topics + LANES
    vocab_total = VOC_DEV * lax.axis_size("dp") * lax.axis_size("vocab")
    step, middle = code_range(flat, topics)
    params = pltpu.CompilerParams(vmem_limit_bytes=16 * 1024 * 1024)
    vmem, hbm = pl.BlockSpec(memory_space=pltpu.VMEM), pl.BlockSpec(memory_space=pltpu.HBM)
    row_shape = jax.ShapeDtypeStruct((8, flat), F32)

    weight = resp_weight.reshape(flat, topics)
    sent = pl.pallas_call(
        prepare_kernel,
        out_shape=jax.ShapeDtypeStruct((flat, wide), BF),
        in_specs=[hbm, hbm, hbm],
        out_specs=hbm,
        scratch_shapes=[pltpu.VMEM((slots, owners), I32)] * 2
        + [
            pltpu.VMEM((flat, topics), BF),
            pltpu.VMEM((flat, LANES), BF),
            pltpu.SemaphoreType.DMA((5,)),
        ],
        compiler_params=pltpu.CompilerParams(vmem_limit_bytes=60 * 1024 * 1024),
        cost_estimate=cost(4 * 8 * flat * topics, 4 * flat * topics),
        name="prepare",
    )(slot_word.T, slot_count.T, weight)
    arrived = lax.all_to_all(
        sent.reshape(owners, slots, wide), "dp", split_axis=0, concat_axis=0, tiled=True
    ).reshape(flat, wide)

    doc_partial, local_rows = pl.pallas_call(
        doc_kernel,
        out_shape=(jax.ShapeDtypeStruct((DOCS, topics), F32), row_shape),
        compiler_params=pltpu.CompilerParams(vmem_limit_bytes=60 * 1024 * 1024),
        cost_estimate=cost(2 * 2 * DOCS * flat * topics, 2 * flat * topics),
        name="doc_counts",
    )(slot_count.T, slot_doc.T, weight)
    docs_own = docs_scatter(doc_partial, topics)
    docs_own = jnp.concatenate([docs_own, jnp.zeros((DOCS // 8, LANES), F32)], axis=1)
    docs_all = lax.all_gather(docs_own, "vocab", axis=0, tiled=True)

    code, group_sums = pl.pallas_call(
        lambda *refs: owner_kernel(step, middle, slots, *refs),
        out_shape=(
            jax.ShapeDtypeStruct((flat, topics), jnp.int16),
            jax.ShapeDtypeStruct((8, LANES), F32),
        ),
        in_specs=[vmem, hbm],
        out_specs=(hbm, vmem),
        scratch_shapes=[pltpu.VMEM((flat, topics), jnp.int16), pltpu.SemaphoreType.DMA((4,))],
        compiler_params=params,
        cost_estimate=cost(2 * 2 * flat * flat * topics, 4 * flat * topics),
        name="word_rows",
    )(arrived, docs_all)
    returned = lax.all_to_all(
        code.reshape(owners, slots, topics), "dp", split_axis=0, concat_axis=0, tiled=True
    ).reshape(flat, topics)
    totals = group_sums + swap(group_sums, 0, 1)
    totals = totals + swap(totals, 1, 0) + swap(totals, 2, 0) + swap(totals, 3, 0)

    rows = min(128, flat)
    across = pl.BlockSpec((rows, topics), lambda i: (i, 0))
    factors = pl.pallas_call(
        lambda *refs: factor_kernel(BETA * vocab_total, *refs),
        out_shape=jax.ShapeDtypeStruct((flat, topics), F32),
        grid=(flat // rows,),
        in_specs=[
            pl.BlockSpec((8, rows), lambda i: (0, i)),
            across,
            pl.BlockSpec((DOCS, wide), lambda i: (0, 0)),
            pl.BlockSpec((8, LANES), lambda i: (0, 0)),
        ],
        out_specs=across,
        compiler_params=pltpu.CompilerParams(vmem_limit_bytes=60 * 1024 * 1024),
        cost_estimate=cost(2 * 2 * DOCS * flat * topics, 6 * flat * topics),
        name="factors",
    )(local_rows, weight, docs_all, totals)
    block = 256
    word_topic = pl.pallas_call(
        word_kernel,
        out_shape=jax.ShapeDtypeStruct((VOC_DEV, topics), F32),
        grid=(VOC_DEV // block,),
        in_specs=[pl.BlockSpec((flat, wide), lambda i: (0, 0)), hbm],
        out_specs=pl.BlockSpec((block, topics), lambda i: (i, 0)),
        scratch_shapes=[pltpu.VMEM((LANES, flat), F32)],
        compiler_params=pltpu.CompilerParams(vmem_limit_bytes=60 * 1024 * 1024),
        cost_estimate=cost(2 * 2 * VOC_DEV * flat * topics, 4 * VOC_DEV * topics),
        name="word_counts",
    )(arrived, factors)

    half = pl.BlockSpec((flat // 2, topics), lambda i: (i, 0))
    resp_new = pl.pallas_call(
        lambda *refs: new_kernel(step, *refs),
        out_shape=jax.ShapeDtypeStruct((flat, topics), BF),
        grid=(2,),
        in_specs=[half, half],
        out_specs=half,
        compiler_params=params,
        cost_estimate=cost(8 * flat * topics, 8 * flat * topics),
        name="responsibilities",
    )(returned, factors)
    return (resp_new.reshape(owners, slots, topics), word_topic, docs_all[:, :topics])


def solution(mesh):
    return jax.shard_map(
        on_device,
        mesh=mesh,
        in_specs=(P("dp", "vocab"), P("dp", "vocab"), P("dp", "vocab"), P("dp", "vocab", None)),
        out_specs=(P("dp", "vocab", None), P(("dp", "vocab"), None), P("dp", None)),
        check_vma=False,
    )
```
